256 devices in a mesh: dp: 16 (over y, x), expert: 8 (over z), tensor: 2 (over core).
Axes of the slice: x: 4, y: 4, z: 8, core: 2. Of those that a mesh axis runs over, the one named last changes fastest.
Arguments:
- out_grad: bfloat16 [16384, 2048], P(('dp', 'expert'), 'tensor'), may hold values from -6 to 6
- seq_ids: int32 [128, 128], P(('dp', 'expert')), may hold values from 0 to 3, never falling along the last dimension, each value on 1 to 64 neighbouring positions
- seq_weights: float32 [128, 4], P(('dp', 'expert')), may hold values from -1.5 to 1.5
- expert_ids: int32 [16384, 2], P(('dp', 'expert')), may hold values from 0 to 7, all different within a row; in each aligned block of 128 rows (0 to 127, 128 to 255, ...) at most 48 rows name the same one
- route_probs: bfloat16 [16384, 2], P(('dp', 'expert')), may hold values from 0.19921875 to 1
- down_weight: bfloat16 [8, 7168, 2048], P('expert', ('dp', 'tensor')), may hold values from -0.0625 to 0.0625
- gate_pre: bfloat16 [8, 7168, 6144], P('expert', ('dp', 'tensor')), may hold values from -6 to 6
- up_pre: bfloat16 [8, 7168, 6144], P('expert', ('dp', 'tensor')), may hold values from -6 to 6
Outputs:
- grad_gate: bfloat16 [8, 7168, 6144], P('expert', ('dp', 'tensor'))
- grad_up: bfloat16 [8, 7168, 6144], P('expert', ('dp', 'tensor'))
- grad_down: bfloat16 [8, 7168, 2048], P('expert', ('dp', 'tensor'))
- grad_probs: float32 [16384, 2], P(('dp', 'expert'))
The draws below stay inside these ranges and needn't reach their ends.
Inputs may be any that keep to these rules, and one draw needn't show every extreme that they name: `expert_ids`: the two experts of a token differ. Among the 128 tokens of one shard no expert is named more than 48 times, and in every draw some expert is named exactly 48 times by the tokens of some shard. `seq_ids`: along a shard's row the ids never fall; each of the 4 ids names 1 to 64 tokens of the row, and one names exactly 64.
All inputs are finite; a program needn't handle non-finite values.
Results may differ from the reference program's by a relative error of at most 0.0064.
Values may be sent and summed in bfloat16 or wider, within the bound.
No kernel may reach another device: no remote copies, remote signals or barrier semaphores. Data moves between devices by JAX's collectives and lax.ppermute only.
A program may use at most 128 MiB of HBM per device.

```python
import math
import jax
import jax.numpy as jnp
import numpy as np
from jax import lax

D = 2048
FF = 7168
TOK_DEV = 128
SEQ_DEV = 4
EXPERTS = 8
SHARDS = 128
TOKENS = 16384
CAP = 48
SLOTS = 6144


def shard_levels(stream_key, dims, cuts, least, high):
    level, own = 1.0, jax.random.fold_in(stream_key, 6)
    for axis_at, shards_of in cuts:
        heights = jnp.exp(jax.random.uniform(jax.random.fold_in(own, axis_at), (shards_of,), jnp.float32, least / len(cuts), high / len(cuts)))
        level = level * jnp.repeat(heights, dims[axis_at] // shards_of).reshape([-1 if axis == axis_at else 1 for axis in range(len(dims))])
    return level


def length_profile(amount, total, reach, slope):
    loads = [(1 << 20) // math.isqrt(grade ** slope) + 1 for grade in range(2, amount + 1)]
    spare, counts = total - reach - (amount - 1), [1] * (amount - 1)
    while spare > 0:
        candidates = [i for i in range(amount - 1) if counts[i] < reach]
        mass, budget = sum([loads[i] for i in candidates]), spare
        for i in candidates:
            more = min(reach - counts[i], max(1, budget * loads[i] // mass), spare)
            counts[i] = counts[i] + more
            spare = spare - more
    return np.array([reach] + counts)


def ragged(rng, amount, total, bound, slope):
    if amount == 2:
        one = jax.random.randint(rng, (), max(1, total - bound), min(bound, total - 1) + 1)
        return jnp.stack([one, total - one])
    lengths = jnp.asarray(length_profile(amount, total, bound, slope), jnp.int32)
    pairs = (amount - 1) // 2
    giver, receiver = lengths[1:1 + 2 * pairs:2], lengths[2:2 + 2 * pairs:2]
    slack = jnp.minimum(giver - 1, bound - receiver)
    shifted = jax.random.randint(jax.random.fold_in(rng, 1), (pairs,), 0, 1 << 20) % (slack + 1)
    lengths = lengths.at[1:1 + 2 * pairs:2].set(giver - shifted).at[2:2 + 2 * pairs:2].set(receiver + shifted)
    return lengths[jax.random.permutation(jax.random.fold_in(rng, 2), amount)]


def shared_out(stream_key, own, number, rows, amount, top, limit, skew):
    ranking = jax.random.permutation(stream_key, amount)
    heavy_load, ordinary = load_shares(amount, rows * top, limit, skew, True), load_shares(amount, rows * top, limit, skew, False)
    places = jnp.arange(amount)

    def named(lengths, offset_by):
        used = int((lengths > 0).sum())
        fixed = max(1, used // 4)
        moved = fixed + (places - fixed + offset_by * (used - fixed)) % max(1, amount - fixed)
        return jnp.zeros((amount,), jnp.int32).at[ranking[jnp.where(places < fixed, places, moved)]].set(jnp.asarray(lengths, jnp.int32))

    lengths = jnp.where(number % 4 == 0, named(heavy_load, number // 4), named(ordinary, number - number // 4 - 1))
    mixed = jax.random.permutation(jax.random.fold_in(own, 3), amount)
    giver, sink = mixed[0:amount // 2 * 2:2], mixed[1:amount // 2 * 2:2]
    slack = jnp.minimum(lengths[giver] - 1, limit - lengths[sink]) // 2
    slack = jnp.where((giver == ranking[0]) | (sink == ranking[0]) | (lengths[sink] == 0), 0, jnp.maximum(slack, 0))
    moved = jax.random.randint(jax.random.fold_in(own, 4), (amount // 2,), 0, 1 << 20) % (slack + 1)
    lengths = lengths.at[giver].add(-moved).at[sink].add(moved)
    labels = jnp.searchsorted(jnp.cumsum(lengths), jnp.arange(rows * top), side="right").astype(jnp.int32)
    listing = labels.reshape(top, rows).T
    listing = listing[jax.random.permutation(jax.random.fold_in(own, 1), rows)]
    offset_by = jax.random.randint(jax.random.fold_in(own, 2), (rows, 1), 0, top)
    return jnp.take_along_axis(listing, (jnp.arange(top)[None, :] + offset_by) % top, axis=1)


def load_shares(count, total, bound, slope, full):
    loads = [(1 << 20) // math.isqrt(rank ** slope) + 1 for rank in range(1, count + 1)]
    largest = bound if full else min(bound, max(-(-total // count), total * loads[0] // sum(loads)))
    least = 1 if total - largest >= count - 1 else 0
    given, rest = [largest] + [least] * (count - 1), total - largest - least * (count - 1)
    while rest > 0:
        movable = [i for i in range(1, count) if given[i] < largest] or [i for i in range(1, count) if given[i] < bound]
        mass, left = sum([loads[i] for i in movable]), rest
        for i in movable:
            addition = min(bound - given[i], max(1, left * loads[i] // mass), rest)
            given[i] = given[i] + addition
            rest = rest - addition
    return np.array(given)


def gaussian(own_key, shape, scale, most, cuts=(), held_as=jnp.bfloat16):
    drawn = jax.random.normal(own_key, shape, jnp.float32) * scale
    if len(cuts) > 0:
        drawn = shard_levels(own_key, shape, cuts, -0.22, 0.18) * drawn
    return jnp.clip(drawn, min=-most, max=most).astype(held_as)


def setup_inputs(seed: int = 0) -> dict:
    key_list = jax.random.split(jax.random.key(seed), 9)
    out_grad = gaussian(key_list[0], (TOKENS, D), 0.5, 6.0, ((0, 128), (1, 2)))
    seq_ids = jax.vmap(lambda own: jnp.searchsorted(jnp.cumsum(ragged(own, SEQ_DEV, TOK_DEV, TOK_DEV // 2, 0)), jnp.arange(TOK_DEV), side="right"))(jax.random.split(key_list[1], SHARDS)).reshape((SHARDS, TOK_DEV)).astype(jnp.int32)
    seq_weights = jnp.clip(jax.random.uniform(key_list[2], (SHARDS, SEQ_DEV), jnp.float32, -1.5, 1.5) * shard_levels(key_list[2], (SHARDS, SEQ_DEV), ((0, 128),), -0.4, 0.0), -1.5, 1.5)
    expert_ids_keys = jax.random.split(jax.random.fold_in(key_list[3], 1), TOKENS // TOK_DEV)
    expert_ids_turns = jax.random.permutation(jax.random.fold_in(key_list[3], 3), TOKENS // TOK_DEV)
    expert_ids = jax.vmap(lambda own, number: shared_out(jax.random.fold_in(key_list[3], 2), own, number, TOK_DEV, EXPERTS, 2, CAP, 2))(expert_ids_keys, expert_ids_turns).reshape((TOKENS, 2))
    route_probs = jnp.clip(0.19921875 + 0.80078125 * jax.random.uniform(key_list[4], (TOKENS, 2), jnp.float32) ** shard_levels(key_list[4], (TOKENS, 2), ((0, 128),), -0.2, 0.2), 0.19921875, 1.0).astype(jnp.bfloat16)
    down_weight = gaussian(key_list[5], (EXPERTS, FF, D), FF ** -0.5, 0.0625, ((0, 8), (1, 32)))
    gate_pre = gaussian(key_list[6], (EXPERTS, FF, SLOTS), 1.0, 6.0, ((0, 8), (1, 32)))
    up_pre = gaussian(key_list[7], (EXPERTS, FF, SLOTS), 1.0, 6.0, ((0, 8), (1, 32)))
    return {"out_grad": out_grad, "seq_ids": seq_ids, "seq_weights": seq_weights, "expert_ids": expert_ids, "route_probs": route_probs, "down_weight": down_weight, "gate_pre": gate_pre, "up_pre": up_pre}


def silu_parts(pre_act):
    logistic = jax.nn.sigmoid(pre_act)
    return pre_act * logistic, logistic * (1.0 + pre_act * (1.0 - logistic))


def reference(out_grad, seq_ids, seq_weights, expert_ids, route_probs, down_weight, gate_pre, up_pre):
    shards = seq_ids.shape[0]
    token_count = seq_ids.shape[1]
    experts = down_weight.shape[0]
    capacity = gate_pre.shape[2] // shards
    feature_width = out_grad.shape[1]
    weight_tok = jnp.take_along_axis(seq_weights, seq_ids, axis=1).reshape(-1)
    scaled = (weight_tok[:, None] * out_grad.astype(jnp.float32)).astype(jnp.bfloat16)
    chosen = expert_ids.reshape(shards, 2 * token_count)
    onehot = (chosen[:, :, None] == jnp.arange(experts, dtype=jnp.int32)[None, None, :]).astype(jnp.int32)
    earlier = (jnp.cumsum(onehot, axis=1) - onehot).astype(jnp.int32)
    position = jnp.sum(earlier * onehot, axis=2).astype(jnp.int32)
    slot_index = (jnp.arange(shards, dtype=jnp.int32)[:, None] * capacity + position).reshape(-1).astype(jnp.int32)
    chosen_flat = chosen.reshape(-1).astype(jnp.int32)
    pair_rows = jnp.repeat(scaled, 2, axis=0)
    prob_flat = route_probs.reshape(-1)
    row_table = jnp.zeros((experts, shards * capacity, feature_width), jnp.bfloat16).at[chosen_flat, slot_index].set(pair_rows)
    prob_table = jnp.zeros((experts, shards * capacity), jnp.bfloat16).at[chosen_flat, slot_index].set(prob_flat)

    def per_expert(operands):
        expert_rows, expert_probs, expert_weight, gate_block, up_block = operands
        activated, derivative = silu_parts(gate_block.astype(jnp.float32))
        up_float = up_block.astype(jnp.float32)
        hidden = (activated * up_float).astype(jnp.bfloat16)
        upstream = lax.dot_general(expert_weight, expert_rows, (((1,), (1,)), ((), ())), preferred_element_type=jnp.float32)
        probe_part = jnp.sum(upstream * hidden.astype(jnp.float32), axis=0)
        factor = expert_probs.astype(jnp.float32)[None, :]
        grad_hidden = factor * upstream
        gate_out = (grad_hidden * up_float * derivative).astype(jnp.bfloat16)
        up_out = (grad_hidden * activated).astype(jnp.bfloat16)
        weighted = (expert_probs.astype(jnp.float32)[:, None] * expert_rows.astype(jnp.float32)).astype(jnp.bfloat16)
        down_out = jnp.dot(hidden, weighted, preferred_element_type=jnp.float32).astype(jnp.bfloat16)
        return gate_out, up_out, down_out, probe_part

    grad_gate, grad_up, grad_down, probe = lax.map(per_expert, (row_table, prob_table, down_weight, gate_pre, up_pre))
    grad_probs = probe[chosen_flat, slot_index].reshape(-1, 2)
    return grad_gate, grad_up, grad_down, grad_probs
```

```python
import functools

import jax
import jax.numpy as jnp
from jax import lax
from jax.experimental import pallas as pl
from jax.experimental.pallas import tpu as pltpu
from jax.sharding import PartitionSpec as P

SIDE = 4
NT = (((1,), (1,)), ((), ()))
VMEM = pl.BlockSpec(memory_space=pltpu.VMEM)
SMEM = pl.BlockSpec(memory_space=pltpu.SMEM)
ANY = pl.BlockSpec(memory_space=pl.ANY)
LIMIT = 40 * 1024 * 1024


def params():
    return pltpu.CompilerParams(vmem_limit_bytes=LIMIT)


def cost(flops, bytes_accessed):
    return pl.CostEstimate(flops=int(flops), bytes_accessed=int(bytes_accessed), transcendentals=0)


def pack_kernel(z_ref, grad_ref, seq_ref, sw_ref, ids_ref, probs_ref, *outs):
    experts, cap = len(outs), outs[0].shape[0]
    tokens = grad_ref.shape[0]
    seq = seq_ref[...]
    weight = jnp.zeros((tokens, 1), jnp.float32)
    for j in range(sw_ref.shape[1]):
        weight = weight + jnp.where(seq == j, sw_ref[0, j], 0.0)
    scaled = (weight * grad_ref[...].astype(jnp.float32)).astype(jnp.bfloat16).astype(jnp.float32)
    z = z_ref[0]
    chosen = [ids_ref[k : k + 1, :] for k in range(2)]
    expert_row = lax.broadcasted_iota(jnp.int32, (experts, tokens), 0)
    hits = [(c == expert_row).astype(jnp.float32) for c in chosen]
    before = lax.broadcasted_iota(jnp.int32, (tokens, tokens), 0) < lax.broadcasted_iota(
        jnp.int32, (tokens, tokens), 1
    )
    earlier = jnp.dot(
        (hits[0] + hits[1]).astype(jnp.bfloat16),
        before.astype(jnp.bfloat16),
        preferred_element_type=jnp.float32,
    )
    row = lax.broadcasted_iota(jnp.int32, (experts * cap, tokens), 0)
    total = None
    for k in range(2):
        pos = jnp.sum(hits[k] * earlier, axis=0, keepdims=True).astype(jnp.int32)
        relative = lax.rem(chosen[k] - z + experts, experts) * cap + pos
        pick = (row == relative).astype(jnp.bfloat16)
        rows = (probs_ref[:, k : k + 1].astype(jnp.float32) * scaled).astype(jnp.bfloat16)
        part = jnp.dot(pick, rows, preferred_element_type=jnp.float32)
        total = part if total is None else total + part
    total = total.astype(jnp.bfloat16)
    for k in range(experts):
        outs[k][...] = total[k * cap : (k + 1) * cap]


def pack(z, grad, seq, sw, ids, probs, experts, cap):
    width = grad.shape[1]
    return pl.pallas_call(
        pack_kernel,
        in_specs=[SMEM, VMEM, VMEM, SMEM, VMEM, VMEM],
        out_specs=[VMEM] * experts,
        out_shape=[jax.ShapeDtypeStruct((cap, width), jnp.bfloat16)] * experts,
        compiler_params=params(),
        cost_estimate=cost(2 * experts * cap * 256 * width, 4 * experts * cap * width),
        name="pack",
    )(z, grad, seq, sw, ids, probs)


def order_kernel(e_ref, *refs):
    *chunks, out = refs
    experts, cap = len(chunks), chunks[0].shape[0]
    for k in range(experts):
        source = lax.rem(e_ref[0] - k + experts, experts)
        out[pl.ds(pl.multiple_of(source * cap, 16), cap), :] = chunks[k][...]


def in_order(e, chunks):
    cap, width = chunks[0].shape
    rows = cap * len(chunks)
    return pl.pallas_call(
        order_kernel,
        in_specs=[SMEM] + [VMEM] * len(chunks),
        out_specs=VMEM,
        out_shape=jax.ShapeDtypeStruct((rows, width), jnp.bfloat16),
        compiler_params=params(),
        cost_estimate=cost(0, 4 * rows * width),
        name="in_order",
    )(e, *chunks)


def shifts(first, second):
    pairs = []
    for y in range(SIDE):
        for x in range(SIDE):
            me = y * SIDE + x
            a = ((y + second) % SIDE) * SIDE + (x + first) % SIDE
            b = ((y + first) % SIDE) * SIDE + (x + second) % SIDE
            pairs += [(2 * me, 2 * a), (2 * me + 1, 2 * b + 1)]
    return pairs


def hop(array, first, second):
    return lax.ppermute(array, ("dp", "tensor"), shifts(first, second))


def swap(array):
    return lax.ppermute(array, "tensor", [(0, 1), (1, 0)])


def other_kernel(w_ref, *refs):
    *blocks, out = refs
    for i, block in enumerate(blocks):
        out[i] = lax.dot_general(
            w_ref[...], block[...], NT, preferred_element_type=jnp.float32
        ).astype(jnp.bfloat16)


def for_other(weight, blocks):
    f, width = weight.shape
    rows = blocks[0].shape[0]
    n = len(blocks)
    return pl.pallas_call(
        other_kernel,
        in_specs=[VMEM] * (n + 1),
        out_specs=VMEM,
        out_shape=jax.ShapeDtypeStruct((n, f, rows), jnp.bfloat16),
        compiler_params=params(),
        cost_estimate=cost(2 * n * f * width * rows, 2 * n * rows * width),
        name="for_other",
    )(weight, *blocks)


def down_kernel(n, first, ids_ref, own_ref, other_ref, *refs):
    blocks, refs = refs[:n], refs[n:]
    acc = refs[-1]
    i = pl.program_id(0)
    f = own_ref.shape[0]

    @pl.when(i == 0)
    def _():
        acc[...] = jnp.zeros_like(acc) if first else refs[0][...]

    for j in range(n):

        @pl.when(i == j)
        def _(j=j):
            acc[:f] += jnp.dot(own_ref[...], blocks[j][...], preferred_element_type=jnp.float32)
            acc[f:] += jnp.dot(other_ref[...], blocks[j][...], preferred_element_type=jnp.float32)


def whole(shape):
    return pl.BlockSpec(shape, lambda i, ids: (0,) * len(shape))


def down(ids, own, other, blocks, acc):
    f = own.shape[0]
    rows, width = blocks[0].shape
    n = len(blocks)
    first = acc is None
    column = pl.BlockSpec((f, rows), lambda i, ids: (0, ids[i]))
    total = whole((2 * f, width))
    return pl.pallas_call(
        functools.partial(down_kernel, n, first),
        grid_spec=pltpu.PrefetchScalarGridSpec(
            num_scalar_prefetch=1,
            grid=(n,),
            in_specs=[column, column] + [whole((rows, width))] * n + ([] if first else [total]),
            out_specs=total,
        ),
        out_shape=jax.ShapeDtypeStruct((2 * f, width), jnp.float32),
        input_output_aliases={} if first else {3 + n: 0},
        compiler_params=params(),
        cost_estimate=cost(4 * n * f * width * rows, 2 * n * rows * width + 8 * f * width),
        name="down",
    )(ids, own, other, *blocks, *([] if first else [acc]))


def act_kernel(n, where, groups, ids_ref, w_ref, gate_ref, up_ref, *refs):
    blocks, parts = refs[:n], refs[n : n + groups]
    gate_out, up_out, probe_out = refs[-3:]
    i = pl.program_id(0)
    for j in range(n):

        @pl.when(i == j)
        def _(j=j):
            upstream = lax.dot_general(
                w_ref[...], blocks[j][...], NT, preferred_element_type=jnp.float32
            )
            group, at = where[j]
            upstream = upstream + parts[group][at].astype(jnp.float32)
            gate = gate_ref[...].astype(jnp.float32)
            up = up_ref[...].astype(jnp.float32)
            logistic = 1.0 / (1.0 + jnp.exp(-gate))
            activated = gate * logistic
            derivative = logistic * (1.0 + gate * (1.0 - logistic))
            hidden = (activated * up).astype(jnp.bfloat16).astype(jnp.float32)
            gate_out[...] = (upstream * up * derivative).astype(jnp.bfloat16)
            up_out[...] = (upstream * activated).astype(jnp.bfloat16)
            probe_out[0] = jnp.sum(upstream * hidden, axis=0, keepdims=True)


def act(ids, weight, gate, up, blocks, parts, where, held):
    f = gate.shape[0]
    rows, width = blocks[0].shape
    n, groups = len(blocks), len(parts)
    column = pl.BlockSpec((f, rows), lambda i, ids: (0, ids[i]))
    first = held is None
    base = 4 + n + groups
    return pl.pallas_call(
        functools.partial(act_kernel, n, where, groups),
        grid_spec=pltpu.PrefetchScalarGridSpec(
            num_scalar_prefetch=1,
            grid=(n,),
            in_specs=[whole((f, width)), column, column]
            + [whole((rows, width))] * n
            + [whole(p.shape) for p in parts]
            + ([] if first else [ANY] * 3),
            out_specs=[column, column, pl.BlockSpec((1, 1, rows), lambda i, ids: (ids[i], 0, 0))],
        ),
        out_shape=[
            jax.ShapeDtypeStruct(gate.shape, jnp.bfloat16),
            jax.ShapeDtypeStruct(gate.shape, jnp.bfloat16),
            jax.ShapeDtypeStruct((gate.shape[1] // rows, 1, rows), jnp.float32),
        ],
        input_output_aliases={} if first else {base + t: t for t in range(3)},
        compiler_params=params(),
        cost_estimate=cost(
            2 * n * f * width * rows + 30 * n * f * rows, 2 * n * rows * width + 8 * n * f * rows
        ),
        name="act",
    )(ids, weight, gate, up, *blocks, *parts, *([] if first else held))


GROUPS = (
    ((0, 0), (1, 0), (-1, 0), (2, 0)),
    ((0, 1), (0, -1), (1, 1), (1, -1)),
    ((-1, 1), (-1, -1), (0, 2), (1, 2)),
    ((2, 1), (2, -1)),
    ((-1, 2), (2, 2)),
)
READY = (
    (1, ((0, 0), (1, 0), (-1, 0), (0, 1), (0, -1), (1, 1))),
    (2, ((1, -1), (-1, 1), (-1, -1), (2, 0), (0, 2))),
    (3, ((2, 1), (1, 2))),
    (4, ((-1, 2), (2, -1), (2, 2))),
)


def multicast(block):
    half = block.shape[0] // 2
    b = {(0, 0): block}
    b[1, 0] = hop(block, 1, 0)
    b[-1, 0] = hop(block, -1, 0)
    low = hop(b[1, 0][:half], 1, 0)
    high = hop(b[-1, 0][half:], -1, 0)
    b[2, 0] = jnp.concatenate([low, high], axis=0)
    for a in (0, 1, -1):
        b[a, 1] = hop(b[a, 0], 0, 1)
        b[a, -1] = hop(b[a, 0], 0, -1)
    b[0, 2] = hop(b[0, 1], 0, 1)
    b[1, 2] = hop(b[1, -1], 0, -1)
    b[2, 1] = hop(b[2, 0], 0, 1)
    b[2, -1] = hop(b[2, 0], 0, -1)
    b[-1, 2] = hop(b[-1, 1], 0, 1)
    b[2, 2] = hop(b[2, -1], 0, -1)
    return b


def local(out_grad, seq_ids, seq_weights, expert_ids, route_probs, down_weight, gate_pre, up_pre):
    experts = lax.axis_size("expert")
    columns = lax.axis_size("dp")
    tokens = seq_ids.shape[1]
    width = out_grad.shape[1]
    cap = gate_pre.shape[2] // (columns * experts)
    rows = experts * cap
    gate, up, weight = gate_pre[0], up_pre[0], down_weight[0]
    e = lax.axis_index("expert")
    core = lax.axis_index("tensor")
    d = lax.axis_index("dp")
    x, y = d % SIDE, d // SIDE
    e_arr = e.reshape(1).astype(jnp.int32)

    sent = pack(
        e_arr, out_grad, seq_ids.reshape(tokens, 1), seq_weights, expert_ids.T, route_probs,
        experts, cap,
    )
    chunks = [sent[0]] + [
        lax.ppermute(sent[k], "expert", [(i, (i + k) % experts) for i in range(experts)])
        for k in range(1, experts)
    ]

    w_own = lax.dynamic_slice_in_dim(weight, core * width, width, 1)
    w_other = swap(lax.dynamic_slice_in_dim(weight, (1 - core) * width, width, 1))
    gate32 = gate.astype(jnp.float32)
    hidden = (gate32 * jax.nn.sigmoid(gate32) * up.astype(jnp.float32)).astype(jnp.bfloat16)
    hidden_other = swap(hidden)

    block = in_order(e_arr, chunks)
    b = multicast(block)

    def index(label):
        first, second = label
        dx = jnp.where(core == 0, first, second)
        dy = jnp.where(core == 0, second, first)
        return ((y - dy) % SIDE) * SIDE + (x - dx) % SIDE

    def indices(labels):
        return jnp.stack([index(l) for l in labels]).astype(jnp.int32)

    parts = [swap(for_other(w_other, [b[l] for l in labels])) for labels in GROUPS]
    place = {l: (g, i) for g, labels in enumerate(GROUPS) for i, l in enumerate(labels)}

    acc = None
    for labels in GROUPS:
        acc = down(indices(labels), hidden, hidden_other, [b[l] for l in labels], acc)

    held = None
    for _, labels in READY:
        need = sorted({place[s, f][0] for f, s in labels})
        where = [(need.index(place[s, f][0]), place[s, f][1]) for f, s in labels]
        held = act(
            indices(labels), w_own, gate, up, [b[l] for l in labels],
            [parts[g] for g in need], where, held,
        )
    gate_out, up_out, probe = held

    f = gate.shape[0]
    mine = acc[:f].astype(jnp.bfloat16)
    theirs = swap(acc[f:].astype(jnp.bfloat16))
    grad_down = jnp.where(
        core == 0,
        jnp.concatenate([mine, theirs], axis=1),
        jnp.concatenate([theirs, mine], axis=1),
    )

    shared = jnp.sum(lax.all_to_all(probe.reshape(columns, rows), "dp", 0, 0, tiled=True), axis=0)
    totals = lax.all_gather(shared, "tensor").sum(0)
    returned = lax.all_to_all(totals.reshape(experts, cap), "expert", 0, 0, tiled=True)

    chosen = expert_ids.reshape(-1)
    onehot = (chosen[:, None] == jnp.arange(experts, dtype=jnp.int32)[None, :]).astype(jnp.int32)
    earlier = jnp.cumsum(onehot, axis=0) - onehot
    slot = chosen * cap + jnp.sum(earlier * onehot, axis=1)
    grad_probs = returned.reshape(-1)[slot].reshape(tokens, 2) / route_probs.astype(jnp.float32)
    return gate_out[None], up_out[None], grad_down[None], grad_probs


def solution(mesh):
    return jax.shard_map(
        local,
        mesh=mesh,
        in_specs=(
            P(("dp", "expert"), "tensor"),
            P(("dp", "expert"), None),
            P(("dp", "expert"), None),
            P(("dp", "expert"), None),
            P(("dp", "expert"), None),
            P("expert", ("dp", "tensor"), None),
            P("expert", ("dp", "tensor"), None),
            P("expert", ("dp", "tensor"), None),
        ),
        out_specs=(
            P("expert", ("dp", "tensor"), None),
            P("expert", ("dp", "tensor"), None),
            P("expert", ("dp", "tensor"), None),
            P(("dp", "expert"), None),
        ),
        check_vma=False,
    )
```

```python
import functools

import jax
import jax.numpy as jnp
import numpy as np
from jax import lax
from jax.experimental import pallas as pl
from jax.experimental.pallas import tpu as pltpu
from jax.sharding import PartitionSpec as P

SIDE = 4
NT = (((1,), (1,)), ((), ()))
VMEM = pl.BlockSpec(memory_space=pltpu.VMEM)
SMEM = pl.BlockSpec(memory_space=pltpu.SMEM)
ANY = pl.BlockSpec(memory_space=pl.ANY)


def params(mib=8):
    return pltpu.CompilerParams(vmem_limit_bytes=mib * 1024 * 1024)


def cost(flops=1000, bytes_accessed=1000):
    return pl.CostEstimate(flops=int(flops), bytes_accessed=int(bytes_accessed), transcendentals=0)


def pack_kernel(z_ref, grad_ref, seq_ref, sw_ref, ids_ref, probs_ref, *outs):
    *outs, slot_ref = outs
    experts, cap = len(outs), outs[0].shape[0]
    tokens = grad_ref.shape[0]
    seq = seq_ref[...]
    weight = jnp.zeros((1, tokens), jnp.float32)
    for j in range(sw_ref.shape[1]):
        weight = weight + jnp.where(seq == j, sw_ref[0, j], 0.0)
    z = z_ref[0]
    chosen = [ids_ref[k : k + 1, :] for k in range(2)]
    probs = [probs_ref[k : k + 1, :].astype(jnp.float32) for k in range(2)]
    expert_row = lax.broadcasted_iota(jnp.int32, (experts, tokens), 0)
    hits = [(c == expert_row).astype(jnp.float32) for c in chosen]
    before = lax.broadcasted_iota(jnp.int32, (tokens, tokens), 0) < lax.broadcasted_iota(
        jnp.int32, (tokens, tokens), 1
    )
    earlier = jnp.dot(
        (hits[0] + hits[1]).astype(jnp.bfloat16),
        before.astype(jnp.float32).astype(jnp.bfloat16),
        preferred_element_type=jnp.float32,
    )
    row = lax.broadcasted_iota(jnp.int32, (experts * cap, tokens), 0)
    pick = jnp.zeros((experts * cap, tokens), jnp.float32)
    prob = jnp.zeros((experts * cap, tokens), jnp.float32)
    for k in range(2):
        pos = jnp.sum(hits[k] * earlier, axis=0, keepdims=True).astype(jnp.int32)
        slot_ref[k : k + 1, :] = pos
        relative = lax.rem(chosen[k] - z + experts, experts) * cap + pos
        mine = row == relative
        pick = jnp.where(mine, 1.0, pick)
        prob = jnp.where(mine, probs[k], prob)
    slot_weight = jnp.sum(pick * weight, axis=1, keepdims=True)
    slot_prob = jnp.sum(prob, axis=1, keepdims=True)
    rows = jnp.dot(pick.astype(jnp.bfloat16), grad_ref[...], preferred_element_type=jnp.float32)
    rows = (slot_weight * rows).astype(jnp.bfloat16).astype(jnp.float32)
    rows = (slot_prob * rows).astype(jnp.bfloat16)
    for k in range(experts):
        outs[k][...] = rows[k * cap : (k + 1) * cap]


def pack(z, grad, seq, sw, ids, probs, experts, cap):
    tokens, width = grad.shape
    return pl.pallas_call(
        pack_kernel,
        in_specs=[SMEM, VMEM, VMEM, SMEM, VMEM, VMEM],
        out_specs=[VMEM] * (experts + 1),
        out_shape=[jax.ShapeDtypeStruct((cap, width), jnp.bfloat16)] * experts
        + [jax.ShapeDtypeStruct((2, tokens), jnp.int32)],
        compiler_params=params(),
        cost_estimate=cost(),
        name="pack",
    )(z, grad, seq, sw, ids, probs)


def unpack_kernel(table_ref, ids_ref, pos_ref, probs_ref, out_ref):
    experts, cap = table_ref.shape
    tokens = ids_ref.shape[1]
    expert_row = lax.broadcasted_iota(jnp.int32, (experts, tokens), 0)
    cap_row = lax.broadcasted_iota(jnp.int32, (cap, tokens), 0)
    for k in range(2):
        at = (pos_ref[k : k + 1, :] == cap_row).astype(jnp.float32)
        values = jnp.dot(
            table_ref[...], at, preferred_element_type=jnp.float32,
            precision=lax.Precision.HIGHEST,
        )
        value = jnp.sum(
            jnp.where(ids_ref[k : k + 1, :] == expert_row, values, 0.0), axis=0, keepdims=True
        )
        out_ref[k : k + 1, :] = value / probs_ref[k : k + 1, :].astype(jnp.float32)


def unpack(table, ids, pos, probs):
    return pl.pallas_call(
        unpack_kernel,
        in_specs=[VMEM] * 4,
        out_specs=VMEM,
        out_shape=jax.ShapeDtypeStruct(ids.shape, jnp.float32),
        compiler_params=params(),
        name="unpack",
    )(table, ids, pos, probs)


def prepare_kernel(ids_ref, gate_ref, up_ref, w_ref, slope_ref, act_ref, hidden_ref, half_ref):
    gate = gate_ref[...].astype(jnp.float32)
    up = up_ref[...].astype(jnp.float32)
    logistic = 1.0 / (1.0 + jnp.exp(-gate))
    activated = gate * logistic
    slope_ref[...] = (up * logistic * (1.0 + gate * (1.0 - logistic))).astype(jnp.bfloat16)
    act_ref[...] = activated.astype(jnp.bfloat16)
    hidden_ref[...] = (activated * up).astype(jnp.bfloat16)
    half_ref[...] = w_ref[...]


def prepare(ids, gate, up, weight):
    f, slots = gate.shape
    width = weight.shape[1] // 2
    step = 32
    columns = ids.shape[0] - 1
    spec = pl.BlockSpec((step, slots), lambda i, ids: (i, 0))
    return pl.pallas_call(
        prepare_kernel,
        grid_spec=pltpu.PrefetchScalarGridSpec(
            num_scalar_prefetch=1,
            grid=(f // step,),
            in_specs=[
                spec, spec, pl.BlockSpec((step, width), lambda i, ids: (i, 1 - ids[columns]))
            ],
            out_specs=[spec] * 3 + [pl.BlockSpec((step, width), lambda i, ids: (i, 0))],
        ),
        out_shape=[jax.ShapeDtypeStruct(gate.shape, jnp.bfloat16)] * 3
        + [jax.ShapeDtypeStruct((f, width), jnp.bfloat16)],
        compiler_params=params(10),
        cost_estimate=cost(4000 * 1000 * 1000, 10 * f * slots),
        name="prepare",
    )(ids, gate, up, weight)


def order_kernel(e_ref, *refs):
    *chunks, out = refs
    experts, cap = len(chunks), chunks[0].shape[0]
    for k in range(experts):
        source = lax.rem(e_ref[0] - k + experts, experts)
        out[pl.ds(pl.multiple_of(source * cap, 16), cap), :] = chunks[k][...]


def in_order(e, chunks):
    cap, width = chunks[0].shape
    rows = cap * len(chunks)
    return pl.pallas_call(
        order_kernel,
        in_specs=[SMEM] + [VMEM] * len(chunks),
        out_specs=VMEM,
        out_shape=jax.ShapeDtypeStruct((rows, width), jnp.bfloat16),
        compiler_params=params(),
        cost_estimate=cost(),
        name="in_order",
    )(e, *chunks)


def shifts(first, second):
    pairs = []
    for y in range(SIDE):
        for x in range(SIDE):
            me = y * SIDE + x
            a = ((y + second) % SIDE) * SIDE + (x + first) % SIDE
            b = ((y + first) % SIDE) * SIDE + (x + second) % SIDE
            pairs += [(2 * me, 2 * a), (2 * me + 1, 2 * b + 1)]
    return pairs


def hop(array, first, second):
    return lax.ppermute(array, ("dp", "tensor"), shifts(first, second))


def swap(array):
    return lax.ppermute(array, "tensor", [(0, 1), (1, 0)])


def other_kernel(w_ref, *refs):
    *blocks, out = refs
    for i, block in enumerate(blocks):
        out[i] = lax.dot_general(
            w_ref[...], block[...], NT, preferred_element_type=jnp.float32
        ).astype(jnp.bfloat16)


def for_other(weight, blocks):
    f, width = weight.shape
    rows = blocks[0].shape[0]
    n = len(blocks)
    return pl.pallas_call(
        other_kernel,
        in_specs=[VMEM] * (n + 1),
        out_specs=VMEM,
        out_shape=jax.ShapeDtypeStruct((n, f, rows), jnp.bfloat16),
        compiler_params=params(10),
        cost_estimate=cost(),
        name="for_other",
    )(weight, *blocks)


def down_kernel(n, start, first, last, ids_ref, own_ref, other_ref, *refs):
    blocks, refs = refs[:n], refs[n:]
    both = refs[-1]
    f = own_ref.shape[0]
    rows, width = blocks[0].shape
    for j in range(n):
        column = pl.ds(pl.multiple_of(ids_ref[start + j] * rows, 128), rows)
        both[:f, j * rows : (j + 1) * rows] = own_ref[:, column]
        both[f:, j * rows : (j + 1) * rows] = other_ref[:, column]
    tile = 512

    @pl.loop(0, width // tile)
    def _(t):
        part = pl.ds(pl.multiple_of(t * tile, tile), tile)
        total = jnp.dot(
            both[...],
            jnp.concatenate([block[:, part] for block in blocks], axis=0),
            preferred_element_type=jnp.float32,
        )
        if not first:
            total = total + refs[0][:, part]
        if last:
            mine_ref, theirs_ref = refs[1 - first : 3 - first]
            mine_ref[:, part] = total[:f].astype(jnp.bfloat16)
            theirs_ref[:, part] = total[f:].astype(jnp.bfloat16)
        else:
            refs[1 - first][:, part] = total


def down(ids, start, own, other, blocks, acc, last):
    f = own.shape[0]
    rows, width = blocks[0].shape
    n = len(blocks)
    first = acc is None
    half = jax.ShapeDtypeStruct((f, width), jnp.bfloat16)
    return pl.pallas_call(
        functools.partial(down_kernel, n, start, first, last),
        in_specs=[SMEM] + [VMEM] * (2 + n + (not first)),
        out_specs=[VMEM, VMEM] if last else VMEM,
        out_shape=[half, half] if last else jax.ShapeDtypeStruct((2 * f, width), jnp.float32),
        scratch_shapes=[pltpu.VMEM((2 * f, n * rows), jnp.bfloat16)],
        compiler_params=params(16),
        cost_estimate=cost(2000 * 1000 * 1000, 1000) if last else cost(),
        name="down",
    )(ids, in_vmem(own), in_vmem(other), *blocks, *([] if first else [acc]))


def finish_kernel(ids_ref, mine_ref, theirs_ref, out_ref):
    core = ids_ref[ids_ref.shape[0] - 1]
    width = mine_ref.shape[1]
    out_ref[:, pl.ds(pl.multiple_of(core * width, 128), width)] = mine_ref[...]
    out_ref[:, pl.ds(pl.multiple_of((1 - core) * width, 128), width)] = theirs_ref[...]


def finish(ids, mine, theirs):
    f, width = mine.shape
    return pl.pallas_call(
        finish_kernel,
        in_specs=[SMEM, VMEM, VMEM],
        out_specs=VMEM,
        out_shape=jax.ShapeDtypeStruct((f, 2 * width), mine.dtype),
        compiler_params=params(),
        cost_estimate=cost(),
        name="finish",
    )(ids, mine, theirs)


def act_kernel(n, start, where, groups, ids_ref, w_ref, slope_ref, act_ref, hidden_ref, *refs):
    blocks, parts = refs[:n], refs[n : n + groups]
    gate_out, up_out, probe_out, gate_buf, up_buf, weight, sems = refs[-7:]
    rows, width = blocks[0].shape
    core = ids_ref[ids_ref.shape[0] - 1]
    load = pltpu.make_async_copy(
        w_ref.at[:, pl.ds(pl.multiple_of(core * width, 128), width)], weight, sems.at[2, 0]
    )
    load.start()
    load.wait()

    def copies(j):
        column = pl.ds(pl.multiple_of(ids_ref[start + j] * rows, 128), rows)
        return (
            pltpu.make_async_copy(gate_buf.at[j], gate_out.at[:, column], sems.at[0, j]),
            pltpu.make_async_copy(up_buf.at[j], up_out.at[:, column], sems.at[1, j]),
        )

    for j in range(n):
        upstream = lax.dot_general(
            weight[...], blocks[j][...], NT, preferred_element_type=jnp.float32
        )
        group, at = where[j]
        upstream = upstream + parts[group][at].astype(jnp.float32)
        column = pl.ds(pl.multiple_of(ids_ref[start + j] * rows, 128), rows)
        gate_buf[j] = (upstream * slope_ref[:, column].astype(jnp.float32)).astype(jnp.bfloat16)
        up_buf[j] = (upstream * act_ref[:, column].astype(jnp.float32)).astype(jnp.bfloat16)
        for copy in copies(j):
            copy.start()
        probe_out[ids_ref[start + j]] = jnp.sum(
            upstream * hidden_ref[:, column].astype(jnp.float32), axis=0, keepdims=True
        )
    for j in range(n):
        for copy in copies(j):
            copy.wait()


def act(ids, start, weight, slope, activated, hidden, blocks, parts, where, held):
    f, slots = slope.shape
    rows = blocks[0].shape[0]
    n, groups = len(blocks), len(parts)
    first = held is None
    base = 5 + n + groups
    return pl.pallas_call(
        functools.partial(act_kernel_first if first else act_kernel_next, n, start, where, groups),
        in_specs=[SMEM, ANY] + [VMEM] * (3 + n + groups) + ([] if first else [ANY, ANY, VMEM]),
        out_specs=[ANY, ANY, VMEM],
        out_shape=[
            jax.ShapeDtypeStruct((f, slots), jnp.bfloat16),
            jax.ShapeDtypeStruct((f, slots), jnp.bfloat16),
            jax.ShapeDtypeStruct((slots // rows, 1, rows), jnp.float32),
        ],
        scratch_shapes=[
            pltpu.VMEM((n, f, rows), jnp.bfloat16),
            pltpu.VMEM((n, f, rows), jnp.bfloat16),
            pltpu.VMEM((f, blocks[0].shape[1]), jnp.bfloat16),
            pltpu.SemaphoreType.DMA((3, n)),
        ],
        input_output_aliases={} if first else {base: 0, base + 1: 1},
        compiler_params=params(16),
        cost_estimate=cost(),
        name="act",
    )(ids, in_hbm(weight), in_vmem(slope), in_vmem(activated), in_vmem(hidden), *blocks, *parts, *([] if first else held))


def act_kernel_first(*args):
    act_kernel(*args)


def act_kernel_next(n, start, where, groups, *refs):
    inputs = refs[: 5 + n + groups]
    held_probe, probe_out = refs[5 + n + groups + 2], refs[-5]
    probe_out[...] = held_probe[...]
    act_kernel(n, start, where, groups, *inputs, *refs[-7:])


def in_hbm(array):
    return pltpu.with_memory_space_constraint(array, pltpu.HBM)


def in_vmem(array):
    return pltpu.with_memory_space_constraint(array, pltpu.VMEM)


def after(array, *others):
    return lax.optimization_barrier((array, *others))[0]


ACT = (
    ((0, 0), (1, 0), (-1, 0), (0, 1), (0, -1)),
    ((1, 1), (1, -1), (-1, 1), (-1, -1)),
    ((2, 0), (0, 2), (2, 1), (1, 2)),
    ((-1, 2), (2, -1), (2, 2)),
)
OTHER = (
    ((0, 0), (1, 0), (-1, 0), (0, 1), (0, -1)),
    ((2, 0), (1, 1), (1, -1)),
    ((-1, 1), (-1, -1), (2, 1), (2, -1)),
    ((0, 2), (1, 2)),
    ((-1, 2), (2, 2)),
)
LABELS = sum(ACT, ())
PLACE = {label: (g, i) for g, labels in enumerate(OTHER) for i, label in enumerate(labels)}


def index_table():
    table = np.zeros((2 * SIDE * SIDE, len(LABELS) + 1), np.int32)
    for device in range(2 * SIDE * SIDE):
        core, x, y = device % 2, device // 2 % SIDE, device // 2 // SIDE
        for i, (first, second) in enumerate(LABELS):
            dx, dy = (second, first) if core else (first, second)
            table[device, i] = (y - dy) % SIDE * SIDE + (x - dx) % SIDE
        table[device, -1] = core
    return table


def local(out_grad, seq_ids, seq_weights, expert_ids, route_probs, down_weight, gate_pre, up_pre):
    experts = lax.axis_size("expert")
    columns = lax.axis_size("dp")
    width = out_grad.shape[1]
    cap = gate_pre.shape[2] // (columns * experts)
    rows = experts * cap
    weight = down_weight[0]
    core = lax.axis_index("tensor")
    e_arr = lax.axis_index("expert").reshape(1).astype(jnp.int32)
    ids = lax.dynamic_index_in_dim(
        jnp.asarray(index_table()), lax.axis_index("dp") * 2 + core, 0, keepdims=False
    )

    *sent, pos = pack(
        after(e_arr, ids), in_hbm(out_grad), in_hbm(seq_ids), seq_weights, in_hbm(expert_ids.T),
        in_hbm(route_probs.T), experts, cap
    )
    chunks = [sent[0]] + [
        lax.ppermute(sent[k], "expert", [(i, (i + k) % experts) for i in range(experts)])
        for k in range(1, experts)
    ]
    slope, activated, hidden, w_send = prepare(
        ids, in_hbm(gate_pre[0]), in_hbm(after(up_pre[0], pos)), in_hbm(weight)
    )
    block = in_order(after(e_arr, hidden), [in_hbm(c) for c in chunks])
    w_other = swap(after(w_send, block))
    hidden_other = swap(after(hidden, block))

    b = {(0, 0): block}
    parts, held = [], None

    def other():
        parts.append(swap(for_other(w_other, [b[l] for l in OTHER[len(parts)]])))

    def activate(step, held):
        labels = ACT[step]
        need = sorted({PLACE[s, f][0] for f, s in labels})
        where = [(need.index(PLACE[s, f][0]), PLACE[s, f][1]) for f, s in labels]
        start = sum(len(a) for a in ACT[:step])
        return act(
            ids, start, weight, slope, activated, hidden, [b[l] for l in labels],
            [parts[g] for g in need], where, held,
        )

    def send_both(first, source):
        b[first, 1] = hop(source, 0, 1)
        b[first, -1] = hop(source, 0, -1)

    b[1, 0] = hop(block, 1, 0)
    b[-1, 0] = hop(block, -1, 0)
    send_both(0, block)
    b[2, 0] = hop(b[1, 0], 1, 0)
    send_both(1, b[1, 0])
    send_both(-1, after(b[-1, 0], b[0, 1], b[0, -1]))
    raw = for_other(w_other, [b[l] for l in OTHER[0]])
    parts.append(swap(raw))
    send_both(2, after(b[2, 0], raw, b[1, 1], b[1, -1]))
    held = activate(0, held)
    b[0, 2] = hop(after(b[0, 1], b[-1, 1], held[2]), 0, 1)
    b[1, 2] = hop(after(b[1, -1], b[-1, 1], held[2]), 0, -1)
    raw = for_other(w_other, [b[l] for l in OTHER[1]])
    parts.append(swap(raw))
    acc = down(ids, 0, hidden, hidden_other, [b[l] for l in ACT[0]], None, False)
    b[-1, 2] = hop(after(b[-1, 1], raw, acc, b[2, 1]), 0, 1)
    b[2, 2] = hop(after(b[2, -1], raw, acc, b[2, 1]), 0, -1)
    raw = for_other(w_other, [b[l] for l in OTHER[2]])
    parts.append(swap(raw))
    held = activate(1, held)
    raw = for_other(w_other, [b[l] for l in OTHER[3]])
    parts.append(swap(raw))
    held = activate(2, held)
    middle = ACT[1] + ACT[2]
    acc = down(ids, len(ACT[0]), hidden, hidden_other, [b[l] for l in middle], acc, False)
    last = after(b[-1, 2], held[2], acc)
    raw = for_other(w_other, [last, b[2, 2]])
    parts.append(swap(raw))
    blocks = [after(b[ACT[3][0]], raw)] + [b[l] for l in ACT[3][1:]]
    mine, theirs = down(
        ids, len(ACT[0] + middle), hidden, hidden_other, blocks, acc, True
    )
    gate_out, up_out, probe = activate(3, held)
    grad_down = finish(ids, mine, swap(after(theirs, probe)))

    shared = jnp.sum(lax.all_to_all(probe.reshape(columns, rows), "dp", 0, 0, tiled=True), axis=0)
    totals = lax.all_gather(shared, "tensor").sum(0)
    returned = lax.all_to_all(totals.reshape(experts, cap), "expert", 0, 0, tiled=True)
    grad_probs = unpack(returned, expert_ids.T, pos, route_probs.T).T
    return gate_out[None], up_out[None], grad_down[None], grad_probs


def solution(mesh):
    return jax.shard_map(
        local,
        mesh=mesh,
        in_specs=(
            P(("dp", "expert"), "tensor"),
            P(("dp", "expert"), None),
            P(("dp", "expert"), None),
            P(("dp", "expert"), None),
            P(("dp", "expert"), None),
            P("expert", ("dp", "tensor"), None),
            P("expert", ("dp", "tensor"), None),
            P("expert", ("dp", "tensor"), None),
        ),
        out_specs=(
            P("expert", ("dp", "tensor"), None),
            P("expert", ("dp", "tensor"), None),
            P("expert", ("dp", "tensor"), None),
            P(("dp", "expert"), None),
        ),
        check_vma=False,
    )
```

```python
import functools

import jax
import jax.numpy as jnp
import numpy as np
from jax import lax
from jax.experimental import pallas as pl
from jax.experimental.pallas import tpu as pltpu
from jax.sharding import PartitionSpec as P

SIDE = 4
NT = (((1,), (1,)), ((), ()))
VMEM = pl.BlockSpec(memory_space=pltpu.VMEM)
SMEM = pl.BlockSpec(memory_space=pltpu.SMEM)
ANY = pl.BlockSpec(memory_space=pl.ANY)


def params(mib=8):
    return pltpu.CompilerParams(vmem_limit_bytes=mib * 1024 * 1024)


def cost(flops=1000, bytes_accessed=1000):
    return pl.CostEstimate(flops=int(flops), bytes_accessed=int(bytes_accessed), transcendentals=0)


def pack_kernel(z_ref, grad_ref, seq_ref, sw_ref, ids_ref, probs_ref, *outs):
    *outs, slot_ref = outs
    experts, cap = len(outs), outs[0].shape[0]
    tokens = grad_ref.shape[0]
    seq = seq_ref[...]
    weight = jnp.zeros((1, tokens), jnp.float32)
    for j in range(sw_ref.shape[1]):
        weight = weight + jnp.where(seq == j, sw_ref[0, j], 0.0)
    z = z_ref[0]
    chosen = [ids_ref[k : k + 1, :] for k in range(2)]
    probs = [probs_ref[k : k + 1, :].astype(jnp.float32) for k in range(2)]
    expert_row = lax.broadcasted_iota(jnp.int32, (experts, tokens), 0)
    hits = [(c == expert_row).astype(jnp.float32) for c in chosen]
    before = lax.broadcasted_iota(jnp.int32, (tokens, tokens), 0) < lax.broadcasted_iota(
        jnp.int32, (tokens, tokens), 1
    )
    earlier = jnp.dot(
        (hits[0] + hits[1]).astype(jnp.bfloat16),
        before.astype(jnp.float32).astype(jnp.bfloat16),
        preferred_element_type=jnp.float32,
    )
    row = lax.broadcasted_iota(jnp.int32, (experts * cap, tokens), 0)
    pick = jnp.zeros((experts * cap, tokens), jnp.float32)
    prob = jnp.zeros((experts * cap, tokens), jnp.float32)
    for k in range(2):
        pos = jnp.sum(hits[k] * earlier, axis=0, keepdims=True).astype(jnp.int32)
        slot_ref[k : k + 1, :] = pos
        relative = lax.rem(chosen[k] - z + experts, experts) * cap + pos
        mine = row == relative
        pick = jnp.where(mine, 1.0, pick)
        prob = jnp.where(mine, probs[k], prob)
    slot_weight = jnp.sum(pick * weight, axis=1, keepdims=True)
    slot_prob = jnp.sum(prob, axis=1, keepdims=True)
    rows = jnp.dot(pick.astype(jnp.bfloat16), grad_ref[...], preferred_element_type=jnp.float32)
    rows = (slot_weight * rows).astype(jnp.bfloat16).astype(jnp.float32)
    rows = (slot_prob * rows).astype(jnp.bfloat16)
    for k in range(experts):
        outs[k][...] = rows[k * cap : (k + 1) * cap]


def pack(z, grad, seq, sw, ids, probs, experts, cap):
    tokens, width = grad.shape
    return pl.pallas_call(
        pack_kernel,
        in_specs=[SMEM, VMEM, VMEM, SMEM, VMEM, VMEM],
        out_specs=[VMEM] * (experts + 1),
        out_shape=[jax.ShapeDtypeStruct((cap, width), jnp.bfloat16)] * experts
        + [jax.ShapeDtypeStruct((2, tokens), jnp.int32)],
        compiler_params=params(),
        cost_estimate=cost(),
        name="pack",
    )(z, grad, seq, sw, ids, probs)


def unpack_kernel(table_ref, ids_ref, pos_ref, probs_ref, out_ref):
    experts, cap = table_ref.shape
    tokens = ids_ref.shape[1]
    expert_row = lax.broadcasted_iota(jnp.int32, (experts, tokens), 0)
    cap_row = lax.broadcasted_iota(jnp.int32, (cap, tokens), 0)
    for k in range(2):
        at = (pos_ref[k : k + 1, :] == cap_row).astype(jnp.float32)
        values = jnp.dot(
            table_ref[...], at, preferred_element_type=jnp.float32,
            precision=lax.Precision.HIGHEST,
        )
        value = jnp.sum(
            jnp.where(ids_ref[k : k + 1, :] == expert_row, values, 0.0), axis=0, keepdims=True
        )
        out_ref[k : k + 1, :] = value / probs_ref[k : k + 1, :].astype(jnp.float32)


def unpack(table, ids, pos, probs):
    return pl.pallas_call(
        unpack_kernel,
        in_specs=[VMEM] * 4,
        out_specs=VMEM,
        out_shape=jax.ShapeDtypeStruct(ids.shape, jnp.float32),
        compiler_params=params(),
        name="unpack",
    )(table, ids, pos, probs)


def prepare_kernel(ids_ref, gate_ref, up_ref, w_ref, slope_ref, act_ref, give_ref, keep_ref):
    core = ids_ref[ids_ref.shape[0] - 1]
    slots, width = gate_ref.shape[1], keep_ref.shape[1]
    gate = gate_ref[...].astype(jnp.float32)
    up = up_ref[...].astype(jnp.float32)
    logistic = 1.0 / (1.0 + jnp.exp(-gate))
    activated = gate * logistic
    slope_ref[...] = (up * logistic * (1.0 + gate * (1.0 - logistic))).astype(jnp.bfloat16)
    act_ref[...] = activated.astype(jnp.bfloat16)
    give_ref[:, :slots] = (activated * up).astype(jnp.bfloat16)
    give_ref[:, slots:] = w_ref[:, pl.ds(pl.multiple_of((1 - core) * width, 128), width)]
    keep_ref[...] = w_ref[:, pl.ds(pl.multiple_of(core * width, 128), width)]


def prepare(ids, gate, up, weight):
    f, slots = gate.shape
    width = weight.shape[1] // 2
    step = 32

    def rows_of(columns):
        return pl.BlockSpec((step, columns), lambda i, ids: (i, 0))

    return pl.pallas_call(
        prepare_kernel,
        grid_spec=pltpu.PrefetchScalarGridSpec(
            num_scalar_prefetch=1,
            grid=(f // step,),
            in_specs=[rows_of(slots), rows_of(slots), rows_of(2 * width)],
            out_specs=[rows_of(slots), rows_of(slots), rows_of(slots + width), rows_of(width)],
        ),
        out_shape=[
            jax.ShapeDtypeStruct((f, columns), jnp.bfloat16)
            for columns in (slots, slots, slots + width, width)
        ],
        compiler_params=params(10),
        cost_estimate=cost(4000 * 1000 * 1000, 10 * f * slots),
        name="prepare",
    )(ids, gate, up, weight)


def join_kernel(a_ref, b_ref, out_ref):
    rows = a_ref.shape[0]
    out_ref[:rows] = a_ref[...]
    out_ref[rows:] = b_ref[...]


def join(a, b):
    rows, width = a.shape
    return pl.pallas_call(
        join_kernel,
        in_specs=[VMEM, VMEM],
        out_specs=VMEM,
        out_shape=jax.ShapeDtypeStruct((2 * rows, width), a.dtype),
        compiler_params=params(),
        cost_estimate=cost(),
        name="join",
    )(a, b)


def order_kernel(e_ref, *refs):
    *chunks, out = refs
    experts, cap = len(chunks), chunks[0].shape[0]
    for k in range(experts):
        source = lax.rem(e_ref[0] - k + experts, experts)
        out[pl.ds(pl.multiple_of(source * cap, 16), cap), :] = chunks[k][...]


def in_order(e, chunks):
    cap, width = chunks[0].shape
    rows = cap * len(chunks)
    return pl.pallas_call(
        order_kernel,
        in_specs=[SMEM] + [VMEM] * len(chunks),
        out_specs=VMEM,
        out_shape=jax.ShapeDtypeStruct((rows, width), jnp.bfloat16),
        compiler_params=params(),
        cost_estimate=cost(),
        name="in_order",
    )(e, *chunks)


def shifts(first, second):
    pairs = []
    for y in range(SIDE):
        for x in range(SIDE):
            me = y * SIDE + x
            a = ((y + second) % SIDE) * SIDE + (x + first) % SIDE
            b = ((y + first) % SIDE) * SIDE + (x + second) % SIDE
            pairs += [(2 * me, 2 * a), (2 * me + 1, 2 * b + 1)]
    return pairs


def hop(array, first, second):
    return lax.ppermute(array, ("dp", "tensor"), shifts(first, second))


def swap(array):
    return lax.ppermute(array, "tensor", [(0, 1), (1, 0)])


def distinct(blocks):
    arrays, at = [], []
    for array, row in blocks:
        if not any(array is other for other in arrays):
            arrays.append(array)
        at.append(([array is other for other in arrays].index(True), row))
    return arrays, at


def other_kernel(at, rows, give_ref, *refs):
    *arrays, out = refs
    width = arrays[0].shape[1]
    weight = give_ref[:, give_ref.shape[1] - width :]
    for i, (which, row) in enumerate(at):
        out[i] = lax.dot_general(
            weight, arrays[which][row : row + rows], NT, preferred_element_type=jnp.float32
        ).astype(jnp.bfloat16)


def for_other(given, rows, blocks):
    f = given.shape[0]
    arrays, at = distinct(blocks)
    return pl.pallas_call(
        functools.partial(other_kernel, at, rows),
        in_specs=[VMEM] * (1 + len(arrays)),
        out_specs=VMEM,
        out_shape=jax.ShapeDtypeStruct((len(at), f, rows), jnp.bfloat16),
        compiler_params=params(10),
        cost_estimate=cost(),
        name="for_other",
    )(in_vmem(given), *arrays)


def down_kernel(at, n, rows, start, first, last, ids_ref, own_ref, other_ref, *refs):
    arrays, refs = refs[:n], refs[n:]
    both = refs[-1]
    f = own_ref.shape[0]
    width = arrays[0].shape[1]
    for j in range(len(at)):
        column = pl.ds(pl.multiple_of(ids_ref[start + j] * rows, 128), rows)
        both[:f, j * rows : (j + 1) * rows] = own_ref[:, column]
        both[f:, j * rows : (j + 1) * rows] = other_ref[:, column]
    tile = 512

    @pl.loop(0, width // tile)
    def _(t):
        part = pl.ds(pl.multiple_of(t * tile, tile), tile)
        total = jnp.dot(
            both[...],
            jnp.concatenate([arrays[w][row : row + rows, part] for w, row in at], axis=0),
            preferred_element_type=jnp.float32,
        )
        if not first:
            total = total + refs[0][:, part]
        if last:
            mine_ref, theirs_ref = refs[1 - first : 3 - first]
            mine_ref[:, part] = total[:f].astype(jnp.bfloat16)
            theirs_ref[:, part] = total[f:].astype(jnp.bfloat16)
        else:
            refs[1 - first][:, part] = total


def down(ids, start, own, other, rows, blocks, acc, last):
    f = own.shape[0]
    arrays, at = distinct(blocks)
    n, width = len(arrays), arrays[0].shape[1]
    first = acc is None
    half = jax.ShapeDtypeStruct((f, width), jnp.bfloat16)
    return pl.pallas_call(
        functools.partial(down_kernel, at, n, rows, start, first, last),
        in_specs=[SMEM] + [VMEM] * (2 + n + (not first)),
        out_specs=[VMEM, VMEM] if last else VMEM,
        out_shape=[half, half] if last else jax.ShapeDtypeStruct((2 * f, width), jnp.float32),
        scratch_shapes=[pltpu.VMEM((2 * f, len(at) * rows), jnp.bfloat16)],
        compiler_params=params(16),
        cost_estimate=cost(2000 * 1000 * 1000, 1000) if last else cost(),
        name="down",
    )(ids, in_vmem(own), in_vmem(other), *arrays, *([] if first else [acc]))


def finish_kernel(ids_ref, mine_ref, theirs_ref, out_ref):
    core = ids_ref[ids_ref.shape[0] - 1]
    width = mine_ref.shape[1]
    out_ref[:, pl.ds(pl.multiple_of(core * width, 128), width)] = mine_ref[...]
    out_ref[:, pl.ds(pl.multiple_of((1 - core) * width, 128), width)] = theirs_ref[...]


def finish(ids, mine, theirs):
    f, width = mine.shape
    return pl.pallas_call(
        finish_kernel,
        in_specs=[SMEM, VMEM, VMEM],
        out_specs=VMEM,
        out_shape=jax.ShapeDtypeStruct((f, 2 * width), mine.dtype),
        compiler_params=params(),
        cost_estimate=cost(),
        name="finish",
    )(ids, mine, theirs)


def act_kernel(at, n, rows, start, where, groups, ids_ref, *refs):
    weight, slope_ref, act_ref, hidden_ref = refs[:4]
    arrays, parts = refs[4 : 4 + n], refs[4 + n : 4 + n + groups]
    refs = refs[4 + n + groups :]
    gate_out, up_out, probe_out, gate_buf, up_buf, sems = refs[-6:]
    if len(refs) > 6:
        probe_out[...] = refs[2][...]
    copies = []
    for j, (which, row) in enumerate(at):
        column = pl.ds(pl.multiple_of(ids_ref[start + j] * rows, 128), rows)
        group, i = where[j]
        upstream = lax.dot_general(
            weight[...], arrays[which][row : row + rows], NT, preferred_element_type=jnp.float32
        ) + parts[group][i].astype(jnp.float32)
        gate_buf[j] = (upstream * slope_ref[:, column].astype(jnp.float32)).astype(jnp.bfloat16)
        up_buf[j] = (upstream * act_ref[:, column].astype(jnp.float32)).astype(jnp.bfloat16)
        copies += [
            pltpu.make_async_copy(gate_buf.at[j], gate_out.at[:, column], sems.at[0, j]),
            pltpu.make_async_copy(up_buf.at[j], up_out.at[:, column], sems.at[1, j]),
        ]
        for copy in copies[-2:]:
            copy.start()
        probe_out[ids_ref[start + j]] = jnp.sum(
            upstream * hidden_ref[:, column].astype(jnp.float32), axis=0, keepdims=True
        )
    for copy in copies:
        copy.wait()


def act(ids, start, weight, slope, activated, hidden, rows, blocks, parts, where, held):
    f, slots = slope.shape
    arrays, at = distinct(blocks)
    n, groups = len(arrays), len(parts)
    first = held is None
    base = 5 + n + groups
    return pl.pallas_call(
        functools.partial(act_kernel, at, n, rows, start, where, groups),
        in_specs=[SMEM] + [VMEM] * (4 + n + groups) + ([] if first else [ANY, ANY, VMEM]),
        out_specs=[ANY, ANY, VMEM],
        out_shape=[
            jax.ShapeDtypeStruct((f, slots), jnp.bfloat16),
            jax.ShapeDtypeStruct((f, slots), jnp.bfloat16),
            jax.ShapeDtypeStruct((slots // rows, 1, rows), jnp.float32),
        ],
        scratch_shapes=[
            pltpu.VMEM((len(at), f, rows), jnp.bfloat16),
            pltpu.VMEM((len(at), f, rows), jnp.bfloat16),
            pltpu.SemaphoreType.DMA((2, len(at))),
        ],
        input_output_aliases={} if first else {base: 0, base + 1: 1},
        compiler_params=params(16),
        cost_estimate=cost(),
        name="act",
    )(
        ids, in_vmem(weight), in_vmem(slope), in_vmem(activated), in_vmem(hidden), *arrays,
        *parts, *([] if first else held),
    )


def in_hbm(array):
    return pltpu.with_memory_space_constraint(array, pltpu.HBM)


def in_vmem(array):
    return pltpu.with_memory_space_constraint(array, pltpu.VMEM)


def after(array, *others):
    return lax.optimization_barrier((array, *others))[0]


ACT = (
    ((0, 0), (1, 0), (-1, 0), (0, 1), (0, -1)),
    ((2, 0), (0, 2), (1, 1), (-1, 1), (1, -1), (-1, -1)),
    ((2, 1), (2, -1), (1, 2), (-1, 2), (2, 2)),
)
OTHER = (ACT[0], ACT[1], ((2, 1), (2, -1), (2, 2)), ((1, 2), (-1, 2)))
LABELS = sum(ACT, ())
PLACE = {label: (g, i) for g, labels in enumerate(OTHER) for i, label in enumerate(labels)}


def index_table():
    table = np.zeros((2 * SIDE * SIDE, len(LABELS) + 1), np.int32)
    for device in range(2 * SIDE * SIDE):
        core, x, y = device % 2, device // 2 % SIDE, device // 2 // SIDE
        for i, (first, second) in enumerate(LABELS):
            dx, dy = (second, first) if core else (first, second)
            table[device, i] = (y - dy) % SIDE * SIDE + (x - dx) % SIDE
        table[device, -1] = core
    return table


def local(out_grad, seq_ids, seq_weights, expert_ids, route_probs, down_weight, gate_pre, up_pre):
    experts = lax.axis_size("expert")
    columns = lax.axis_size("dp")
    width = out_grad.shape[1]
    cap = gate_pre.shape[2] // (columns * experts)
    rows = experts * cap
    weight = down_weight[0]
    core = lax.axis_index("tensor")
    e_arr = lax.axis_index("expert").reshape(1).astype(jnp.int32)
    ids = lax.dynamic_index_in_dim(
        jnp.asarray(index_table()), lax.axis_index("dp") * 2 + core, 0, keepdims=False
    )

    *sent, pos = pack(
        after(e_arr, ids), in_hbm(out_grad), in_hbm(seq_ids), seq_weights, in_hbm(expert_ids.T),
        in_hbm(route_probs.T), experts, cap
    )
    arrived = {0: sent[0]}
    half_way = experts // 2
    nearest = (1, experts - 1)
    middle = [k for k in range(2, experts - 1) if abs(k - half_way) > 1]
    for k in nearest + (half_way + 1, half_way, half_way - 1) + tuple(middle):
        chunk = sent[k]
        if k in middle:
            chunk = after(chunk, arrived[nearest[k < half_way]])
        arrived[k] = lax.ppermute(
            chunk, "expert", [(i, (i + k) % experts) for i in range(experts)]
        )
    chunks = [arrived[k] for k in range(experts)]
    slope, activated, give, w_own = prepare(
        ids, in_hbm(gate_pre[0]), in_hbm(after(up_pre[0], pos)), in_hbm(weight)
    )
    block = in_order(after(e_arr, give), [in_hbm(c) for c in chunks])
    got = swap(after(give, block))

    b = {(0, 0): (block, 0)}
    parts, held = [], None

    def share(step, *others):
        blocks = [b[l] for l in OTHER[step]]
        raw = for_other(after(got, *others) if others else got, rows, blocks)
        parts.append(swap(raw))
        return raw

    def activate(step, held):
        labels = ACT[step]
        need = sorted({PLACE[s, f][0] for f, s in labels})
        where = [(need.index(PLACE[s, f][0]), PLACE[s, f][1]) for f, s in labels]
        start = sum(len(a) for a in ACT[:step])
        return act(
            ids, start, w_own, slope, activated, give, rows, [b[l] for l in labels],
            [parts[g] for g in need], where, held,
        )

    def accumulate(step, acc, *others):
        blocks = [b[l] for l in ACT[step]]
        start = sum(len(a) for a in ACT[:step])
        own = after(give, *others) if others else give
        return down(ids, start, own, got, rows, blocks, acc, step == len(ACT) - 1)

    right, left = hop(block, 1, 0), hop(block, -1, 0)
    up_one, down_one = hop(block, 0, 1), hop(block, 0, -1)
    b[1, 0], b[-1, 0], b[0, 1], b[0, -1] = (right, 0), (left, 0), (up_one, 0), (down_one, 0)
    far = hop(right, 1, 0)
    b[2, 0] = (far, 0)
    pair = join(right, left)
    pair_up, pair_down = hop(pair, 0, 1), hop(pair, 0, -1)
    b[1, 1], b[-1, 1] = (pair_up, 0), (pair_up, rows)
    b[1, -1], b[-1, -1] = (pair_down, 0), (pair_down, rows)
    b[0, 2] = (hop(down_one, 0, -1), 0)
    raw = share(0)
    far_up, far_down = hop(after(far, raw), 0, 1), hop(after(far, raw), 0, -1)
    b[2, 1], b[2, -1] = (far_up, 0), (far_down, 0)
    held = activate(0, held)
    acc = accumulate(0, None)
    pair_far = hop(after(pair_up, held[2], acc, far_up), 0, 1)
    b[1, 2], b[-1, 2] = (pair_far, 0), (pair_far, rows)
    b[2, 2] = (hop(far_down, 0, -1), 0)
    share(1)
    held = activate(1, held)
    acc = accumulate(1, acc)
    share(2, held[2], acc)
    raw = share(3, parts[2])
    mine, theirs = accumulate(2, acc, raw)
    gate_out, up_out, probe = activate(2, held)
    grad_down = finish(ids, mine, swap(after(theirs, probe)))

    shared = jnp.sum(lax.all_to_all(probe.reshape(columns, rows), "dp", 0, 0, tiled=True), axis=0)
    totals = lax.all_gather(shared, "tensor").sum(0)
    returned = lax.all_to_all(totals.reshape(experts, cap), "expert", 0, 0, tiled=True)
    grad_probs = unpack(returned, expert_ids.T, pos, route_probs.T).T
    return gate_out[None], up_out[None], grad_down[None], grad_probs


def solution(mesh):
    return jax.shard_map(
        local,
        mesh=mesh,
        in_specs=(
            P(("dp", "expert"), "tensor"),
            P(("dp", "expert"), None),
            P(("dp", "expert"), None),
            P(("dp", "expert"), None),
            P(("dp", "expert"), None),
            P("expert", ("dp", "tensor"), None),
            P("expert", ("dp", "tensor"), None),
            P("expert", ("dp", "tensor"), None),
        ),
        out_specs=(
            P("expert", ("dp", "tensor"), None),
            P("expert", ("dp", "tensor"), None),
            P("expert", ("dp", "tensor"), None),
            P(("dp", "expert"), None),
        ),
        check_vma=False,
    )
```

```python
import functools

import jax
import jax.numpy as jnp
import numpy as np
from jax import lax
from jax.experimental import pallas as pl
from jax.experimental.pallas import tpu as pltpu
from jax.sharding import PartitionSpec as P

SIDE = 4
NT = (((1,), (1,)), ((), ()))
VMEM = pl.BlockSpec(memory_space=pltpu.VMEM)
SMEM = pl.BlockSpec(memory_space=pltpu.SMEM)
ANY = pl.BlockSpec(memory_space=pl.ANY)


def params(mib=8):
    return pltpu.CompilerParams(vmem_limit_bytes=mib * 1024 * 1024)


def cost(flops=1000, bytes_accessed=1000):
    return pl.CostEstimate(flops=int(flops), bytes_accessed=int(bytes_accessed), transcendentals=0)


def pack_kernel(z_ref, grad_ref, seq_ref, sw_ref, ids_ref, probs_ref, *outs):
    *outs, slot_ref = outs
    experts, cap = len(outs), outs[0].shape[0]
    tokens = grad_ref.shape[0]
    seq = seq_ref[...]
    weight = jnp.zeros((1, tokens), jnp.float32)
    for j in range(sw_ref.shape[1]):
        weight = weight + jnp.where(seq == j, sw_ref[0, j], 0.0)
    z = z_ref[0]
    chosen = [ids_ref[k : k + 1, :] for k in range(2)]
    probs = [probs_ref[k : k + 1, :].astype(jnp.float32) for k in range(2)]
    expert_row = lax.broadcasted_iota(jnp.int32, (experts, tokens), 0)
    hits = [(c == expert_row).astype(jnp.float32) for c in chosen]
    before = lax.broadcasted_iota(jnp.int32, (tokens, tokens), 0) < lax.broadcasted_iota(
        jnp.int32, (tokens, tokens), 1
    )
    earlier = jnp.dot(
        (hits[0] + hits[1]).astype(jnp.bfloat16),
        before.astype(jnp.float32).astype(jnp.bfloat16),
        preferred_element_type=jnp.float32,
    )
    row = lax.broadcasted_iota(jnp.int32, (experts * cap, tokens), 0)
    pick = jnp.zeros((experts * cap, tokens), jnp.float32)
    prob = jnp.zeros((experts * cap, tokens), jnp.float32)
    for k in range(2):
        pos = jnp.sum(hits[k] * earlier, axis=0, keepdims=True).astype(jnp.int32)
        slot_ref[k : k + 1, :] = pos
        relative = lax.rem(chosen[k] - z + experts, experts) * cap + pos
        mine = row == relative
        pick = jnp.where(mine, 1.0, pick)
        prob = jnp.where(mine, probs[k], prob)
    slot_weight = jnp.sum(pick * weight, axis=1, keepdims=True)
    slot_prob = jnp.sum(prob, axis=1, keepdims=True)
    rows = jnp.dot(pick.astype(jnp.bfloat16), grad_ref[...], preferred_element_type=jnp.float32)
    rows = (slot_weight * rows).astype(jnp.bfloat16).astype(jnp.float32)
    rows = (slot_prob * rows).astype(jnp.bfloat16)
    for k in range(experts):
        outs[k][...] = rows[k * cap : (k + 1) * cap]


def pack(z, grad, seq, sw, ids, probs, experts, cap):
    tokens, width = grad.shape
    return pl.pallas_call(
        pack_kernel,
        in_specs=[SMEM, VMEM, VMEM, SMEM, VMEM, VMEM],
        out_specs=[VMEM] * (experts + 1),
        out_shape=[jax.ShapeDtypeStruct((cap, width), jnp.bfloat16)] * experts
        + [jax.ShapeDtypeStruct((2, tokens), jnp.int32)],
        compiler_params=params(),
        cost_estimate=cost(),
        name="pack",
    )(z, grad, seq, sw, ids, probs)


def unpack_kernel(table_ref, ids_ref, pos_ref, probs_ref, out_ref):
    experts, cap = table_ref.shape
    tokens = ids_ref.shape[1]
    expert_row = lax.broadcasted_iota(jnp.int32, (experts, tokens), 0)
    cap_row = lax.broadcasted_iota(jnp.int32, (cap, tokens), 0)
    for k in range(2):
        at = (pos_ref[k : k + 1, :] == cap_row).astype(jnp.float32)
        values = jnp.dot(
            table_ref[...], at, preferred_element_type=jnp.float32,
            precision=lax.Precision.HIGHEST,
        )
        value = jnp.sum(
            jnp.where(ids_ref[k : k + 1, :] == expert_row, values, 0.0), axis=0, keepdims=True
        )
        out_ref[k : k + 1, :] = value / probs_ref[k : k + 1, :].astype(jnp.float32)


def unpack(table, ids, pos, probs):
    return pl.pallas_call(
        unpack_kernel,
        in_specs=[VMEM] * 4,
        out_specs=VMEM,
        out_shape=jax.ShapeDtypeStruct(ids.shape, jnp.float32),
        compiler_params=params(),
        name="unpack",
    )(table, ids, pos, probs)


def prepare_kernel(ids_ref, gate_ref, up_ref, w_ref, slope_ref, act_ref, give_ref, keep_ref):
    core = ids_ref[ids_ref.shape[0] - 1]
    slots, width = gate_ref.shape[1], keep_ref.shape[1]
    gate = gate_ref[...].astype(jnp.float32)
    up = up_ref[...].astype(jnp.float32)
    logistic = 1.0 / (1.0 + jnp.exp(-gate))
    activated = gate * logistic
    slope_ref[...] = (up * logistic * (1.0 + gate * (1.0 - logistic))).astype(jnp.bfloat16)
    act_ref[...] = activated.astype(jnp.bfloat16)
    give_ref[:, :slots] = (activated * up).astype(jnp.bfloat16)
    give_ref[:, slots:] = w_ref[:, pl.ds(pl.multiple_of((1 - core) * width, 128), width)]
    keep_ref[...] = w_ref[:, pl.ds(pl.multiple_of(core * width, 128), width)]


def prepare(ids, gate, up, weight):
    f, slots = gate.shape
    width = weight.shape[1] // 2
    step = 32

    def rows_of(columns):
        return pl.BlockSpec((step, columns), lambda i, ids: (i, 0))

    return pl.pallas_call(
        prepare_kernel,
        grid_spec=pltpu.PrefetchScalarGridSpec(
            num_scalar_prefetch=1,
            grid=(f // step,),
            in_specs=[rows_of(slots), rows_of(slots), rows_of(2 * width)],
            out_specs=[rows_of(slots), rows_of(slots), rows_of(slots + width), rows_of(width)],
        ),
        out_shape=[
            jax.ShapeDtypeStruct((f, columns), jnp.bfloat16)
            for columns in (slots, slots, slots + width, width)
        ],
        compiler_params=params(10),
        cost_estimate=cost(4000 * 1000 * 1000, 10 * f * slots),
        name="prepare",
    )(ids, gate, up, weight)


def join_kernel(a_ref, b_ref, out_ref):
    rows = a_ref.shape[0]
    out_ref[:rows] = a_ref[...]
    out_ref[rows:] = b_ref[...]


def join(a, b):
    rows, width = a.shape
    return pl.pallas_call(
        join_kernel,
        in_specs=[VMEM, VMEM],
        out_specs=VMEM,
        out_shape=jax.ShapeDtypeStruct((2 * rows, width), a.dtype),
        compiler_params=params(),
        cost_estimate=cost(),
        name="join",
    )(a, b)


def order_kernel(e_ref, *refs):
    *chunks, out = refs
    experts, cap = len(chunks), chunks[0].shape[0]
    for k in range(experts):
        source = lax.rem(e_ref[0] - k + experts, experts)
        out[pl.ds(pl.multiple_of(source * cap, 16), cap), :] = chunks[k][...]


def in_order(e, chunks):
    cap, width = chunks[0].shape
    rows = cap * len(chunks)
    return pl.pallas_call(
        order_kernel,
        in_specs=[SMEM] + [VMEM] * len(chunks),
        out_specs=VMEM,
        out_shape=jax.ShapeDtypeStruct((rows, width), jnp.bfloat16),
        compiler_params=params(),
        cost_estimate=cost(),
        name="in_order",
    )(e, *chunks)


def shifts(first, second):
    pairs = []
    for y in range(SIDE):
        for x in range(SIDE):
            me = y * SIDE + x
            a = ((y + second) % SIDE) * SIDE + (x + first) % SIDE
            b = ((y + first) % SIDE) * SIDE + (x + second) % SIDE
            pairs += [(2 * me, 2 * a), (2 * me + 1, 2 * b + 1)]
    return pairs


def hop(array, first, second):
    return lax.ppermute(array, ("dp", "tensor"), shifts(first, second))


def swap(array):
    return lax.ppermute(array, "tensor", [(0, 1), (1, 0)])


def distinct(blocks):
    arrays, at = [], []
    for array, row in blocks:
        if not any(array is other for other in arrays):
            arrays.append(array)
        at.append(([array is other for other in arrays].index(True), row))
    return arrays, at


def other_kernel(at, rows, give_ref, *refs):
    *arrays, out = refs
    width = arrays[0].shape[1]
    weight = give_ref[:, give_ref.shape[1] - width :]
    for i, (which, row) in enumerate(at):
        out[i] = lax.dot_general(
            weight, arrays[which][row : row + rows], NT, preferred_element_type=jnp.float32
        ).astype(jnp.bfloat16)


def for_other(given, rows, blocks):
    f = given.shape[0]
    arrays, at = distinct(blocks)
    return pl.pallas_call(
        functools.partial(other_kernel, at, rows),
        in_specs=[VMEM] * (1 + len(arrays)),
        out_specs=VMEM,
        out_shape=jax.ShapeDtypeStruct((len(at), f, rows), jnp.bfloat16),
        compiler_params=params(10),
        cost_estimate=cost(),
        name="for_other",
    )(in_vmem(given), *arrays)


def down_kernel(at, n, rows, start, first, last, ids_ref, own_ref, other_ref, *refs):
    arrays, refs = refs[:n], refs[n:]
    both = refs[-1]
    f = own_ref.shape[0]
    width = arrays[0].shape[1]
    for j in range(len(at)):
        column = pl.ds(pl.multiple_of(ids_ref[start + j] * rows, 128), rows)
        both[:f, j * rows : (j + 1) * rows] = own_ref[:, column]
        both[f:, j * rows : (j + 1) * rows] = other_ref[:, column]
    tile = 512

    @pl.loop(0, width // tile)
    def _(t):
        part = pl.ds(pl.multiple_of(t * tile, tile), tile)
        total = jnp.dot(
            both[...],
            jnp.concatenate([arrays[w][row : row + rows, part] for w, row in at], axis=0),
            preferred_element_type=jnp.float32,
        )
        if not first:
            total = total + refs[0][:, part]
        if last:
            mine_ref, theirs_ref = refs[1 - first : 3 - first]
            mine_ref[:, part] = total[:f].astype(jnp.bfloat16)
            theirs_ref[:, part] = total[f:].astype(jnp.bfloat16)
        else:
            refs[1 - first][:, part] = total


def down(ids, start, own, other, rows, blocks, acc, last):
    f = own.shape[0]
    arrays, at = distinct(blocks)
    n, width = len(arrays), arrays[0].shape[1]
    first = acc is None
    half = jax.ShapeDtypeStruct((f, width), jnp.bfloat16)
    return pl.pallas_call(
        functools.partial(down_kernel, at, n, rows, start, first, last),
        in_specs=[SMEM] + [VMEM] * (2 + n + (not first)),
        out_specs=[VMEM, VMEM] if last else VMEM,
        out_shape=[half, half] if last else jax.ShapeDtypeStruct((2 * f, width), jnp.float32),
        scratch_shapes=[pltpu.VMEM((2 * f, len(at) * rows), jnp.bfloat16)],
        compiler_params=params(16),
        cost_estimate=cost(2000 * 1000 * 1000, 1000) if last else cost(),
        name="down",
    )(ids, in_vmem(own), in_vmem(other), *arrays, *([] if first else [acc]))


def finish_kernel(ids_ref, mine_ref, theirs_ref, out_ref):
    core = ids_ref[ids_ref.shape[0] - 1]
    width = mine_ref.shape[1]
    out_ref[:, pl.ds(pl.multiple_of(core * width, 128), width)] = mine_ref[...]
    out_ref[:, pl.ds(pl.multiple_of((1 - core) * width, 128), width)] = theirs_ref[...]


def finish(ids, mine, theirs):
    f, width = mine.shape
    return pl.pallas_call(
        finish_kernel,
        in_specs=[SMEM, VMEM, VMEM],
        out_specs=VMEM,
        out_shape=jax.ShapeDtypeStruct((f, 2 * width), mine.dtype),
        compiler_params=params(),
        cost_estimate=cost(),
        name="finish",
    )(ids, mine, theirs)


def act_kernel(at, n, rows, start, where, groups, ids_ref, *refs):
    weight, slope_ref, act_ref, hidden_ref = refs[:4]
    arrays, parts = refs[4 : 4 + n], refs[4 + n : 4 + n + groups]
    refs = refs[4 + n + groups :]
    gate_out, up_out, probe_out, gate_buf, up_buf, sems = refs[-6:]
    if len(refs) > 6:
        probe_out[...] = refs[2][...]
    copies = []
    for j, (which, row) in enumerate(at):
        column = pl.ds(pl.multiple_of(ids_ref[start + j] * rows, 128), rows)
        group, i = where[j]
        upstream = lax.dot_general(
            weight[...], arrays[which][row : row + rows], NT, preferred_element_type=jnp.float32
        ) + parts[group][i].astype(jnp.float32)
        gate_buf[j] = (upstream * slope_ref[:, column].astype(jnp.float32)).astype(jnp.bfloat16)
        up_buf[j] = (upstream * act_ref[:, column].astype(jnp.float32)).astype(jnp.bfloat16)
        copies += [
            pltpu.make_async_copy(gate_buf.at[j], gate_out.at[:, column], sems.at[0, j]),
            pltpu.make_async_copy(up_buf.at[j], up_out.at[:, column], sems.at[1, j]),
        ]
        for copy in copies[-2:]:
            copy.start()
        probe_out[ids_ref[start + j]] = jnp.sum(
            upstream * hidden_ref[:, column].astype(jnp.float32), axis=0, keepdims=True
        )
    for copy in copies:
        copy.wait()


def act(ids, start, weight, slope, activated, hidden, rows, blocks, parts, where, held):
    f, slots = slope.shape
    arrays, at = distinct(blocks)
    n, groups = len(arrays), len(parts)
    first = held is None
    base = 5 + n + groups
    return pl.pallas_call(
        functools.partial(act_kernel, at, n, rows, start, where, groups),
        in_specs=[SMEM] + [VMEM] * (4 + n + groups) + ([] if first else [ANY, ANY, VMEM]),
        out_specs=[ANY, ANY, VMEM],
        out_shape=[
            jax.ShapeDtypeStruct((f, slots), jnp.bfloat16),
            jax.ShapeDtypeStruct((f, slots), jnp.bfloat16),
            jax.ShapeDtypeStruct((slots // rows, 1, rows), jnp.float32),
        ],
        scratch_shapes=[
            pltpu.VMEM((len(at), f, rows), jnp.bfloat16),
            pltpu.VMEM((len(at), f, rows), jnp.bfloat16),
            pltpu.SemaphoreType.DMA((2, len(at))),
        ],
        input_output_aliases={} if first else {base: 0, base + 1: 1},
        compiler_params=params(16),
        cost_estimate=cost(),
        name="act",
    )(
        ids, in_vmem(weight), in_vmem(slope), in_vmem(activated), in_vmem(hidden), *arrays,
        *parts, *([] if first else held),
    )


def in_hbm(array):
    return pltpu.with_memory_space_constraint(array, pltpu.HBM)


def in_vmem(array):
    return pltpu.with_memory_space_constraint(array, pltpu.VMEM)


def after(array, *others):
    return lax.optimization_barrier((array, *others))[0]


ACT = (
    ((0, 0), (1, 0), (-1, 0), (0, 1), (0, -1)),
    ((2, 0), (0, 2), (1, 1), (-1, 1), (1, -1), (-1, -1)),
    ((2, 1), (2, -1), (2, 2), (1, 2), (-1, 2)),
)
OTHER = (ACT[0], ACT[1], ((2, 1), (2, -1), (2, 2)), ((1, 2), (-1, 2)))
LABELS = sum(ACT, ())
PLACE = {label: (g, i) for g, labels in enumerate(OTHER) for i, label in enumerate(labels)}


def index_table():
    table = np.zeros((2 * SIDE * SIDE, len(LABELS) + 1), np.int32)
    for device in range(2 * SIDE * SIDE):
        core, x, y = device % 2, device // 2 % SIDE, device // 2 // SIDE
        for i, (first, second) in enumerate(LABELS):
            dx, dy = (second, first) if core else (first, second)
            table[device, i] = (y - dy) % SIDE * SIDE + (x - dx) % SIDE
        table[device, -1] = core
    return table


def local(out_grad, seq_ids, seq_weights, expert_ids, route_probs, down_weight, gate_pre, up_pre):
    experts = lax.axis_size("expert")
    columns = lax.axis_size("dp")
    width = out_grad.shape[1]
    cap = gate_pre.shape[2] // (columns * experts)
    rows = experts * cap
    weight = down_weight[0]
    core = lax.axis_index("tensor")
    e_arr = lax.axis_index("expert").reshape(1).astype(jnp.int32)
    ids = lax.dynamic_index_in_dim(
        jnp.asarray(index_table()), lax.axis_index("dp") * 2 + core, 0, keepdims=False
    )

    *sent, pos = pack(
        after(e_arr, ids), in_hbm(out_grad), in_hbm(seq_ids), seq_weights, in_hbm(expert_ids.T),
        in_hbm(route_probs.T), experts, cap
    )
    arrived = {0: sent[0]}
    half_way = experts // 2
    nearest = (1, experts - 1)
    middle = [k for k in range(2, experts - 1) if abs(k - half_way) > 1]
    for k in nearest + (half_way + 1, half_way, half_way - 1) + tuple(middle):
        chunk = sent[k]
        if k in middle:
            chunk = after(chunk, arrived[nearest[k < half_way]])
        arrived[k] = lax.ppermute(
            chunk, "expert", [(i, (i + k) % experts) for i in range(experts)]
        )
    chunks = [arrived[k] for k in range(experts)]
    slope, activated, give, w_own = prepare(
        ids, in_hbm(gate_pre[0]), in_hbm(after(up_pre[0], pos)), in_hbm(weight)
    )
    block = in_order(after(e_arr, give), [in_hbm(c) for c in chunks])
    got = swap(after(give, block))

    b = {(0, 0): (block, 0)}
    parts, held = [], None

    def share(step, *others):
        blocks = [b[l] for l in OTHER[step]]
        raw = for_other(after(got, *others) if others else got, rows, blocks)
        parts.append(swap(raw))
        return raw

    def activate(step, held):
        labels = ACT[step]
        need = sorted({PLACE[s, f][0] for f, s in labels})
        where = [(need.index(PLACE[s, f][0]), PLACE[s, f][1]) for f, s in labels]
        start = sum(len(a) for a in ACT[:step])
        return act(
            ids, start, w_own, slope, activated, give, rows, [b[l] for l in labels],
            [parts[g] for g in need], where, held,
        )

    def accumulate(labels, acc, last, *others):
        blocks = [b[l] for l in labels]
        own = after(give, *others) if others else give
        return down(ids, LABELS.index(labels[0]), own, got, rows, blocks, acc, last)

    right, left = hop(block, 1, 0), hop(block, -1, 0)
    up_one, down_one = hop(block, 0, 1), hop(block, 0, -1)
    b[1, 0], b[-1, 0], b[0, 1], b[0, -1] = (right, 0), (left, 0), (up_one, 0), (down_one, 0)
    far = hop(right, 1, 0)
    b[2, 0] = (far, 0)
    pair = join(right, left)
    pair_up, pair_down = hop(pair, 0, 1), hop(pair, 0, -1)
    b[1, 1], b[-1, 1] = (pair_up, 0), (pair_up, rows)
    b[1, -1], b[-1, -1] = (pair_down, 0), (pair_down, rows)
    b[0, 2] = (hop(down_one, 0, -1), 0)
    raw = share(0)
    far_up, far_down = hop(after(far, raw), 0, 1), hop(after(far, raw), 0, -1)
    b[2, 1], b[2, -1] = (far_up, 0), (far_down, 0)
    held = activate(0, held)
    acc = accumulate(ACT[0], None, False)
    pair_far = hop(after(pair_up, held[2], acc, far_up), 0, 1)
    b[1, 2], b[-1, 2] = (pair_far, 0), (pair_far, rows)
    b[2, 2] = (hop(far_down, 0, -1), 0)
    share(1)
    held = activate(1, held)
    acc = accumulate(ACT[1] + ACT[2][:2], acc, False)
    share(2, held[2], acc)
    raw = share(3, parts[2])
    mine, theirs = accumulate(ACT[2][2:], acc, True, raw)
    gate_out, up_out, probe = activate(2, held)
    grad_down = finish(ids, mine, swap(after(theirs, probe)))

    shared = jnp.sum(lax.all_to_all(probe.reshape(columns, rows), "dp", 0, 0, tiled=True), axis=0)
    totals = lax.all_gather(shared, "tensor").sum(0)
    returned = lax.all_to_all(totals.reshape(experts, cap), "expert", 0, 0, tiled=True)
    grad_probs = unpack(returned, expert_ids.T, pos, route_probs.T).T
    return gate_out[None], up_out[None], grad_down[None], grad_probs


def solution(mesh):
    return jax.shard_map(
        local,
        mesh=mesh,
        in_specs=(
            P(("dp", "expert"), "tensor"),
            P(("dp", "expert"), None),
            P(("dp", "expert"), None),
            P(("dp", "expert"), None),
            P(("dp", "expert"), None),
            P("expert", ("dp", "tensor"), None),
            P("expert", ("dp", "tensor"), None),
            P("expert", ("dp", "tensor"), None),
        ),
        out_specs=(
            P("expert", ("dp", "tensor"), None),
            P("expert", ("dp", "tensor"), None),
            P("expert", ("dp", "tensor"), None),
            P(("dp", "expert"), None),
        ),
        check_vma=False,
    )
```
